32 devices in a mesh: section: 4 (over y, core), ep: 8 (over z, x).
Axes of the slice: x: 2, y: 2, z: 4, core: 2. Of those that a mesh axis runs over, the one named last changes fastest.
Arguments:
- output_gradient: bfloat16 [4, 256, 7168], P('section', 'ep'), may hold values from -6 to 6
- expert_ids: int32 [4, 256, 8], P('section', 'ep'), may hold values from 0 to 255, as said below
- gate_weights: float32 [4, 256, 8], P('section', 'ep'), may hold values from 0.1 to 1
- stored_preactivations: bfloat16 [4, 192, 2, 1024], P('section', 'ep'), may hold values from -6 to 6
- w_gate: bfloat16 [8192, 7168], P('ep'), may hold values from -0.0625 to 0.0625
- w_up: bfloat16 [8192, 7168], P('ep'), may hold values from -0.0625 to 0.0625
- w_down: bfloat16 [8192, 7168], P('ep'), may hold values from -0.125 to 0.125
Outputs:
- passed_grad: bfloat16 [4, 256, 7168], P('section', 'ep')
- down_grad: bfloat16 [4, 8192, 7168], P('section', 'ep')
The draws below stay inside these ranges and needn't reach their ends.
Inputs may be any that keep to these rules, and one draw needn't show every extreme that they name: `expert_ids`: A token's 8 ids differ. Ids below 4 name the window's experts; of one device's 32 tokens at most 3 name any one of them, and in every section one of them is named by exactly 3 tokens of every device.
All inputs are finite; a program needn't handle non-finite values.
Results may differ from the reference program's by a relative error of at most 0.0049.
Values may be sent and summed in bfloat16 or wider, within the bound.
A program may use at most 128 MiB of HBM per device.

```python
import jax
import jax.numpy as jnp
from jax import lax

D = 7168
H = 2048
ALL_EXPERTS = 256
TOP = 8
EXPERTS = 4
SLOT = 3
TOK_DEV = 32
SECTIONS = 4
TOKENS = 256
GROUP = 2
HID_DEV = 1024
N_EP = 8


def draw_expert_ids(key, part):
    key = jax.random.fold_in(key, 7)
    key_full, key_count, key_rank, key_other, key_shuffle = jax.random.split(key, 5)
    blocks = TOKENS // TOK_DEV
    favored = jax.random.randint(key_full, (SECTIONS, 1, 1), 0, EXPERTS)
    counts = jax.random.randint(key_count, (SECTIONS, blocks, EXPERTS), 0, SLOT + 1)
    counts = jnp.where(jnp.arange(EXPERTS)[None, None, :] == favored, SLOT, counts)
    scores = jax.random.randint(key_rank, (SECTIONS, blocks, EXPERTS, TOK_DEV), 0, 65536) * TOK_DEV + jnp.arange(TOK_DEV)
    ranking = jnp.argsort(jnp.argsort(scores, axis=-1), axis=-1)
    members = ranking < counts[..., None]
    members = jnp.transpose(members, (0, 1, 3, 2)).reshape(SECTIONS, TOKENS, EXPERTS)
    remaining = ALL_EXPERTS - EXPERTS
    other_scores = jax.random.randint(key_other, (SECTIONS, TOKENS, remaining), 0, 65536) * remaining + jnp.arange(remaining)
    top_values, others = lax.top_k(other_scores, TOP)
    others = others + EXPERTS
    columns = jnp.arange(TOP)
    padding = jnp.zeros((SECTIONS, TOKENS, TOP - EXPERTS), dtype=bool)
    members_wide = jnp.concatenate([members, padding], axis=-1)
    chosen = jnp.where(members_wide, columns, others)
    shuffle_scores = jax.random.randint(key_shuffle, (SECTIONS, TOKENS, TOP), 0, 65536) * TOP + columns
    permuted = jnp.argsort(shuffle_scores, axis=-1)
    return jnp.take_along_axis(chosen, permuted, axis=-1).astype(jnp.int32)


def block_scale(rng, shape, shards, low, largest):
    factor_of = 1.0
    for axis_at, parts in shards:
        heights = jax.random.uniform(jax.random.fold_in(jax.random.fold_in(rng, 6), axis_at), (parts,), jnp.float32, low / len(shards), largest / len(shards))
        factor_of = factor_of * jnp.repeat(jnp.exp(heights), shape[axis_at] // parts).reshape((-1,) + (1,) * (len(shape) - 1 - axis_at))
    return factor_of


def bell_draw(own_key, shape, scale, most, shards=(), kind=jnp.bfloat16):
    drawn = jax.random.normal(own_key, shape, jnp.float32) * scale
    if len(shards) > 0:
        drawn = block_scale(own_key, shape, shards, -0.22, 0.18) * drawn
    return jnp.clip(drawn, min=-most, max=most).astype(kind)


def setup_inputs(seed: int = 0) -> dict:
    key_list = jax.random.split(jax.random.key(seed), 8)
    output_gradient = bell_draw(key_list[0], (SECTIONS, TOKENS, D), 1.0, 6.0, ((0, 4), (1, 8)))
    expert_ids = draw_expert_ids(jax.random.fold_in(key_list[7], 71), 0)
    gate_weights = jnp.clip(0.1 + 0.9 * jax.random.uniform(key_list[2], (SECTIONS, TOKENS, TOP), jnp.float32) ** block_scale(key_list[2], (SECTIONS, TOKENS, TOP), ((0, 4), (1, 8)), -0.2, 0.2), 0.1, 1.0)
    stored_preactivations = bell_draw(key_list[3], (SECTIONS, N_EP * N_EP * SLOT, 2, HID_DEV), 1.0, 6.0, ((0, 4), (1, 8)))
    w_gate = bell_draw(key_list[4], (EXPERTS * H, D), D ** -0.5, 0.0625, ((0, 8),))
    w_up = bell_draw(key_list[5], (EXPERTS * H, D), D ** -0.5, 0.0625, ((0, 8),))
    w_down = bell_draw(key_list[6], (EXPERTS * H, D), H ** -0.5, 0.125, ((0, 8),))
    return {"output_gradient": output_gradient, "expert_ids": expert_ids, "gate_weights": gate_weights, "stored_preactivations": stored_preactivations, "w_gate": w_gate, "w_up": w_up, "w_down": w_down}


def route_tables(token_ids, token_gates):
    matches = token_ids[:, :, None] == jnp.arange(EXPERTS, dtype=jnp.int32)
    members = jnp.sum(matches.astype(jnp.int32), axis=1)
    coefficient = jnp.sum(jnp.where(matches, token_gates[:, :, None], jnp.float32(0.0)), axis=1)
    ranking = jnp.cumsum(members, axis=0) - 1
    slot_ids = jnp.arange(SLOT, dtype=jnp.int32)[:, None, None]
    chosen = jnp.logical_and(members[None] == 1, ranking[None] == slot_ids)
    return jnp.transpose(chosen, (2, 0, 1)), coefficient


def reference(output_gradient, expert_ids, gate_weights, stored_preactivations, w_gate, w_up, w_down):
    all_weights = (w_gate, w_up, w_down)
    return run_all(output_gradient, expert_ids, gate_weights, stored_preactivations, all_weights)


def run_all(output_gradient, expert_ids, gate_weights, stored_preactivations, all_weights):
    section_fn = make_section(all_weights)
    grad_in, down_grad = lax.map(section_fn, (output_gradient, expert_ids, gate_weights, stored_preactivations))
    passed_grad = jnp.concatenate([grad_in[1:], jnp.zeros_like(grad_in[:1])], axis=0)
    return passed_grad, down_grad


def make_section(all_weights):
    def section_fn(operands):
        return section_with(operands, all_weights)
    return section_fn


def section_with(operands, all_weights):
    gradient, token_ids, token_gates, saved_section = operands
    w_gate_all, w_up_all, w_down_all = all_weights
    grad_blocks = gradient.reshape(N_EP, TOK_DEV, D)
    chosen, coefficient = jax.vmap(route_tables)(token_ids.reshape(N_EP, TOK_DEV, TOP), token_gates.reshape(N_EP, TOK_DEV, TOP))
    chosen_f = chosen.astype(jnp.float32)
    picked = jnp.einsum('bekt,btd->bekd', chosen_f, grad_blocks.astype(jnp.float32)).astype(jnp.bfloat16)
    saved_all = saved_section.reshape(N_EP, N_EP * SLOT, 2, HID_DEV)
    expert_contribution = jnp.zeros((N_EP, TOK_DEV, D), jnp.float32)
    down_parts = []
    for expert in range(EXPERTS):
        row_block = picked[:, expert].reshape(N_EP * SLOT, D)
        pre_slices = saved_all[expert * GROUP:(expert + 1) * GROUP]
        gate_pre = jnp.transpose(pre_slices[:, :, 0, :], (1, 0, 2)).reshape(N_EP * SLOT, H).astype(jnp.float32)
        up_pre = jnp.transpose(pre_slices[:, :, 1, :], (1, 0, 2)).reshape(N_EP * SLOT, H).astype(jnp.float32)
        sigmoid_gate = jax.nn.sigmoid(gate_pre)
        swish = gate_pre * sigmoid_gate
        down_weight_piece = w_down_all[expert * H:(expert + 1) * H]
        d_hidden = jnp.dot(row_block, down_weight_piece.T, preferred_element_type=jnp.float32)
        hidden = (swish * up_pre).astype(jnp.bfloat16)
        down_parts.append(jnp.dot(hidden.T, row_block, preferred_element_type=jnp.float32).astype(jnp.bfloat16))
        d_gate = (d_hidden * up_pre * sigmoid_gate * (1.0 + gate_pre * (1.0 - sigmoid_gate))).astype(jnp.bfloat16)
        d_up = (d_hidden * swish).astype(jnp.bfloat16)
        gate_slice = w_gate_all[expert * H:(expert + 1) * H].reshape(GROUP, HID_DEV, D).astype(jnp.float32)
        up_slice = w_up_all[expert * H:(expert + 1) * H].reshape(GROUP, HID_DEV, D).astype(jnp.float32)
        partial_terms = jnp.einsum('rgh,ghd->grd', d_gate.reshape(-1, GROUP, HID_DEV).astype(jnp.float32), gate_slice)
        partial_terms = partial_terms + jnp.einsum('rgh,ghd->grd', d_up.reshape(-1, GROUP, HID_DEV).astype(jnp.float32), up_slice)
        partial_terms = partial_terms.astype(jnp.bfloat16)
        accumulated_total = jnp.sum(partial_terms.astype(jnp.float32), axis=0).reshape(N_EP, SLOT, D)
        gate_weighting_factor = chosen_f[:, expert] * coefficient[:, :, expert][:, None, :]
        expert_contribution = expert_contribution + jnp.einsum('psr,psa->pra', gate_weighting_factor, accumulated_total, precision=lax.Precision.HIGHEST)
    grad_in = (grad_blocks.astype(jnp.float32) + expert_contribution).astype(jnp.bfloat16).reshape(TOKENS, D)
    return grad_in, jnp.concatenate(down_parts, axis=0)
```

```python
import functools

import jax
import jax.numpy as jnp
from jax import lax
from jax.experimental import pallas as pl
from jax.experimental.pallas import tpu as pltpu
from jax.sharding import PartitionSpec as P

EXPERTS = 4
SLOT = 3
PAD = 4
FOLD = 4
ROWS = EXPERTS * PAD
WIDE = 256
F32 = jnp.float32
BF16 = jnp.bfloat16


def nt(a, b):
    return lax.dot_general(a, b, (((1,), (1,)), ((), ())), preferred_element_type=F32)


def tn(a, b):
    return lax.dot_general(a, b, (((0,), (0,)), ((), ())), preferred_element_type=F32)


def nn(a, b):
    return lax.dot_general(a, b, (((1,), (0,)), ((), ())), preferred_element_type=F32)


def iota(shape, dim):
    return lax.broadcasted_iota(jnp.int32, shape, dim)


def main_kernel(
    n_dev, n_sec, pieces,
    grad_ref, ids_ref, gates_ref, pre_ref, wg_hbm, wu_hbm, wd_hbm,
    passed_ref, rows_ref, hidden_ref,
    wg, wu, wd, gsend, grecv, part, xsend, xrecv, zsend, zrecv, gbuf, dh, fg, fu, dgate, dup,
    sel, whi, wlo, perm,
    wd_sem, wg_sem, wu_sem,
    gz_s, gz_r, gx_s, gx_r, rx_s, rx_r, rz_s, rz_r, ps_s, ps_r,
):
    slices = n_dev // EXPERTS
    tok = grad_ref.shape[1]
    w = WIDE
    cw = FOLD * w
    j = lax.axis_index("ep")
    s = lax.axis_index("section")
    e = lax.div(j, slices)
    g = lax.rem(j, slices)

    def cols(p):
        return pl.ds(pl.multiple_of(p * cw, cw), cw)

    def wcopy(hbm, vm, sem, p):
        return pltpu.make_async_copy(hbm.at[:, cols(p)], vm.at[:, cols(p)], sem.at[p])

    barrier = pltpu.get_barrier_semaphore()
    for d in range(1, EXPERTS):
        pl.semaphore_signal(barrier, inc=1, device_id={"ep": lax.rem(e + d, EXPERTS) * slices + g},
                            device_id_type=pl.DeviceIdType.MESH)
    for d in range(1, slices):
        pl.semaphore_signal(barrier, inc=1, device_id={"ep": e * slices + lax.rem(g + d, slices)},
                            device_id_type=pl.DeviceIdType.MESH)

    @pl.when(s > 0)
    def _():
        pl.semaphore_signal(barrier, inc=1, device_id={"section": s - 1},
                            device_id_type=pl.DeviceIdType.MESH)

    @pl.when(s < n_sec - 1)
    def _():
        pl.semaphore_signal(barrier, inc=1, device_id={"section": s + 1},
                            device_id_type=pl.DeviceIdType.MESH)

    def issue_down(p, c):
        wcopy(wd_hbm, wd, wd_sem, p).start()
        return c

    def issue_rest(p, c):
        wcopy(wg_hbm, wg, wg_sem, p).start()
        wcopy(wu_hbm, wu, wu_sem, p).start()
        return c

    lax.fori_loop(0, pieces, issue_down, 0)
    lax.fori_loop(0, pieces, issue_rest, 0)

    ids = ids_ref[0]
    gates = gates_ref[0]
    lane = iota((tok, 128), 1)
    member = jnp.zeros((tok, 128), F32)
    coef = jnp.zeros((tok, 128), F32)
    for c in range(ids.shape[1]):
        eq = ids[:, c:c + 1] == lane
        member = member + jnp.where(eq, 1.0, 0.0)
        coef = coef + jnp.where(eq, gates[:, c:c + 1], 0.0)
    tri = jnp.where(iota((tok, tok), 0) >= iota((tok, tok), 1), 1.0, 0.0).astype(BF16)
    rank = nn(tri, member.astype(BF16)) - 1.0
    rank = jnp.where(member == 1.0, rank, -1.0).astype(BF16)
    rank4 = jnp.concatenate([rank] * FOLD, axis=0)
    q = EXPERTS * FOLD * PAD
    qt = FOLD * tok
    i0 = iota((q, 128), 0)
    spread = jnp.where((i0 >> 4) == iota((q, 128), 1), 1.0, 0.0).astype(BF16)
    ri, rj = iota((q, qt), 0), iota((q, qt), 1)
    hit = jnp.logical_and(
        nt(spread, rank4) == (ri & 3).astype(F32),
        jnp.logical_and(((ri >> 2) & 3) == lax.div(rj, tok), (ri & 3) < SLOT),
    )
    sel[...] = jnp.where(hit, 1.0, 0.0).astype(BF16)
    ci, cj = iota((qt, q), 0), iota((qt, q), 1)
    hit_t = jnp.logical_and(
        nt(rank4, spread) == (cj & 3).astype(F32),
        jnp.logical_and(((cj >> 2) & 3) == lax.div(ci, tok), (cj & 3) < SLOT),
    )
    high = coef.astype(BF16)
    low = (coef - high.astype(F32)).astype(BF16)
    whi[...] = jnp.where(hit_t, nt(jnp.concatenate([high] * FOLD, axis=0), spread), 0.0).astype(BF16)
    wlo[...] = jnp.where(hit_t, nt(jnp.concatenate([low] * FOLD, axis=0), spread), 0.0).astype(BF16)
    fi, fj = iota((q, q), 0), iota((q, q), 1)
    perm[...] = jnp.where(
        jnp.logical_and(
            jnp.logical_and((fi >> 4) == ((fj >> 2) & 3), ((fi >> 2) & 3) == (fj >> 4)),
            (fi & 3) == (fj & 3),
        ),
        1.0, 0.0,
    ).astype(BF16)

    def z_copy(src, dst, ss, rs, p, d):
        to = lax.rem(e + d, EXPERTS)
        return pltpu.make_async_remote_copy(
            src_ref=src.at[p, pl.ds(pl.multiple_of(to * ROWS, ROWS), ROWS)],
            dst_ref=dst.at[p, pl.ds(pl.multiple_of(e * ROWS, ROWS), ROWS)],
            send_sem=ss.at[p, d - 1], recv_sem=rs.at[p, d - 1],
            device_id={"ep": to * slices + g}, device_id_type=pl.DeviceIdType.MESH)

    def z_wait(src, dst, ss, rs, p, d):
        frm = lax.rem(e + EXPERTS - d, EXPERTS)
        spot = pl.ds(pl.multiple_of(frm * ROWS, ROWS), ROWS)
        pltpu.make_async_remote_copy(
            src_ref=src.at[p, spot], dst_ref=dst.at[p, spot],
            send_sem=ss.at[p, d - 1], recv_sem=rs.at[p, d - 1],
            device_id={"ep": frm * slices + g}, device_id_type=pl.DeviceIdType.MESH).wait_recv()

    def gx_copy(p, d, row):
        at = rows_ref.at[pl.ds(pl.multiple_of(row * ROWS, ROWS), ROWS), cols(p)]
        return pltpu.make_async_remote_copy(
            src_ref=at, dst_ref=at, send_sem=gx_s.at[p, d - 1], recv_sem=gx_r.at[p, d - 1],
            device_id={"ep": e * slices + lax.rem(g + d, slices)},
            device_id_type=pl.DeviceIdType.MESH)

    def rx_copy(p, d):
        to = lax.rem(g + d, slices)
        return pltpu.make_async_remote_copy(
            src_ref=xsend.at[p, pl.ds(pl.multiple_of(to * ROWS, ROWS), ROWS)],
            dst_ref=xrecv.at[p, d - 1],
            send_sem=rx_s.at[p, d - 1], recv_sem=rx_r.at[p, d - 1],
            device_id={"ep": e * slices + to}, device_id_type=pl.DeviceIdType.MESH)

    def ps_copy(p):
        return pltpu.make_async_remote_copy(
            src_ref=gbuf.at[:, cols(p)], dst_ref=passed_ref.at[:, cols(p)],
            send_sem=ps_s.at[p], recv_sem=ps_r.at[p],
            device_id={"section": lax.rem(s + n_sec - 1, n_sec)},
            device_id_type=pl.DeviceIdType.MESH)

    mine = pl.ds(pl.multiple_of(e * ROWS, ROWS), ROWS)

    def pick(p, c):
        block = grad_ref[0, :, cols(p)]
        stack = jnp.concatenate([block[:, f * w:(f + 1) * w] for f in range(FOLD)], axis=0)
        gsend[p] = nn(sel[...], stack).astype(BF16)
        grecv[p, mine] = gsend[p, mine]
        return c

    lax.fori_loop(0, pieces, pick, 0)

    neighbours = lax.div(s + n_sec - 1, n_sec) + lax.div(2 * n_sec - 2 - s, n_sec)
    pl.semaphore_wait(barrier, EXPERTS - 1 + slices - 1 + neighbours)

    def send_rows(p, c):
        for d in range(1, EXPERTS):
            z_copy(gsend, grecv, gz_s, gz_r, p, d).start()
        return c

    lax.fori_loop(0, pieces, send_rows, 0)

    m = slices * ROWS
    r = n_dev * SLOT
    pi, pj = iota((m, r), 0), iota((m, r), 1)
    source = (((pi >> 2) & 3) * slices + (pi >> 4)) * SLOT + (pi & 3)
    order = jnp.where(jnp.logical_and(source == pj, (pi & 3) < SLOT), 1.0, 0.0).astype(BF16)
    a = nn(order, pre_ref[0, :, 0, :])
    u = nn(order, pre_ref[0, :, 1, :])
    sig = jax.nn.sigmoid(a)
    swish = a * sig
    hidden_ref[...] = (swish * u).astype(BF16)
    fg[...] = u * sig * (1.0 + a * (1.0 - sig))
    fu[...] = swish
    dh[...] = jnp.zeros_like(dh)

    @pl.when(s == n_sec - 1)
    def _():
        passed_ref[...] = jnp.zeros_like(passed_ref)

    lag = 2

    def gather(p, c):
        @pl.when(p < pieces)
        def _():
            for d in range(1, EXPERTS):
                z_wait(gsend, grecv, gz_s, gz_r, p, d)
            flat = nn(perm[...], grecv[p]).astype(BF16)
            rows_ref[pl.ds(pl.multiple_of(g * ROWS, ROWS), ROWS), cols(p)] = jnp.concatenate(
                [flat[f * ROWS:(f + 1) * ROWS] for f in range(FOLD)], axis=1)
            for d in range(1, slices):
                gx_copy(p, d, g).start()

        @pl.when(p >= lag)
        def _():
            t = p - lag
            for d in range(1, slices):
                gx_copy(t, d, lax.rem(g + slices - d, slices)).wait_recv()
            wcopy(wd_hbm, wd, wd_sem, t).wait()
            dh[...] += nt(rows_ref[:, cols(t)], wd[:, cols(t)])
        return c

    lax.fori_loop(0, pieces + lag, gather, 0)

    d_hidden = dh[...]
    dgate[...] = (d_hidden * fg[...]).astype(BF16)
    dup[...] = (d_hidden * fu[...]).astype(BF16)

    lag_x, lag_z = 1, 3

    def give_back(p, c):
        @pl.when(p < pieces)
        def _():
            wcopy(wg_hbm, wg, wg_sem, p).wait()
            wcopy(wu_hbm, wu, wu_sem, p).wait()
            total = nn(dgate[...], wg[:, cols(p)]) + nn(dup[...], wu[:, cols(p)])
            xsend[p] = total.astype(BF16)
            for d in range(1, slices):
                rx_copy(p, d).start()

        @pl.when(jnp.logical_and(p >= lag_x, p < pieces + lag_x))
        def _():
            t = p - lag_x
            acc = xsend[t, pl.ds(pl.multiple_of(g * ROWS, ROWS), ROWS)].astype(F32)
            for d in range(1, slices):
                rx_copy(t, d).wait_recv()
                acc = acc + xrecv[t, d - 1].astype(F32)
            acc = acc.astype(BF16)
            stack = jnp.concatenate([acc[:, f * w:(f + 1) * w] for f in range(FOLD)], axis=0)
            zsend[t] = nn(perm[...], stack).astype(BF16)
            for d in range(1, EXPERTS):
                z_copy(zsend, zrecv, rz_s, rz_r, t, d).start()
            zrecv[t, mine] = zsend[t, mine]

        @pl.when(p >= lag_z)
        def _():
            t = p - lag_z
            for d in range(1, EXPERTS):
                z_wait(zsend, zrecv, rz_s, rz_r, t, d)
            got = zrecv[t]
            terms = nn(whi[...], got) + nn(wlo[...], got)
            wide = jnp.concatenate([terms[f * tok:(f + 1) * tok] for f in range(FOLD)], axis=1)
            gbuf[:, cols(t)] = (grad_ref[0, :, cols(t)].astype(F32) + wide).astype(BF16)

            @pl.when(s > 0)
            def _():
                ps_copy(t).start()
        return c

    lax.fori_loop(0, pieces + lag_z, give_back, 0)

    def drain(p, c):
        for d in range(1, EXPERTS):
            z_copy(gsend, grecv, gz_s, gz_r, p, d).wait_send()
            z_copy(zsend, zrecv, rz_s, rz_r, p, d).wait_send()
        for d in range(1, slices):
            gx_copy(p, d, g).wait_send()
            rx_copy(p, d).wait_send()

        @pl.when(s < n_sec - 1)
        def _():
            ps_copy(p).wait_recv()

        @pl.when(s > 0)
        def _():
            ps_copy(p).wait_send()
        return c

    lax.fori_loop(0, pieces, drain, 0)


def down_kernel(hidden_ref, rows_ref, passed_ref, down_ref, out_ref):
    @pl.when(pl.program_id(0) == 0)
    def _():
        out_ref[...] = passed_ref[...]

    step = FOLD * WIDE
    h = hidden_ref[...]
    for c in range(rows_ref.shape[1] // step):
        down_ref[:, c * step:(c + 1) * step] = tn(h, rows_ref[:, c * step:(c + 1) * step]).astype(BF16)


def on_device(grad, ids, gates, pre, w_gate, w_up, w_down):
    n_dev = lax.axis_size("ep")
    n_sec = lax.axis_size("section")
    slices = n_dev // EXPERTS
    tok, width = grad.shape[1:]
    hid = w_down.shape[0]
    pieces = width // (FOLD * WIDE)
    m = slices * ROWS
    q = EXPERTS * FOLD * PAD
    qt = FOLD * tok
    vmem = pl.BlockSpec(memory_space=pltpu.VMEM)
    hbm = pl.BlockSpec(memory_space=pl.ANY)
    dma = pltpu.SemaphoreType.DMA
    x_n = slices - 1
    z_n = EXPERTS - 1
    passed, rows, hidden = pl.pallas_call(
        functools.partial(main_kernel, n_dev, n_sec, pieces),
        out_shape=(
            jax.ShapeDtypeStruct((tok, width), BF16),
            jax.ShapeDtypeStruct((m, width), BF16),
            jax.ShapeDtypeStruct((m, hid), BF16),
        ),
        in_specs=[vmem, vmem, vmem, vmem, hbm, hbm, hbm],
        out_specs=(vmem, vmem, vmem),
        scratch_shapes=[
            pltpu.VMEM((hid, width), BF16),
            pltpu.VMEM((hid, width), BF16),
            pltpu.VMEM((hid, width), BF16),
            pltpu.VMEM((pieces, q, WIDE), BF16),
            pltpu.VMEM((pieces, q, WIDE), BF16),
            pltpu.VMEM((8, 128), F32),
            pltpu.VMEM((pieces, m, FOLD * WIDE), BF16),
            pltpu.VMEM((pieces, x_n, ROWS, FOLD * WIDE), BF16),
            pltpu.VMEM((pieces, q, WIDE), BF16),
            pltpu.VMEM((pieces, q, WIDE), BF16),
            pltpu.VMEM((tok, width), BF16),
            pltpu.VMEM((m, hid), F32),
            pltpu.VMEM((m, hid), F32),
            pltpu.VMEM((m, hid), F32),
            pltpu.VMEM((m, hid), BF16),
            pltpu.VMEM((m, hid), BF16),
            pltpu.VMEM((q, qt), BF16),
            pltpu.VMEM((qt, q), BF16),
            pltpu.VMEM((qt, q), BF16),
            pltpu.VMEM((q, q), BF16),
            dma((pieces,)), dma((pieces,)), dma((pieces,)),
            dma((pieces, z_n)), dma((pieces, z_n)),
            dma((pieces, x_n)), dma((pieces, x_n)),
            dma((pieces, x_n)), dma((pieces, x_n)),
            dma((pieces, z_n)), dma((pieces, z_n)),
            dma((pieces,)), dma((pieces,)),
        ],
        compiler_params=pltpu.CompilerParams(
            collective_id=0, has_side_effects=True, vmem_limit_bytes=60 * 1024 * 1024),
        cost_estimate=pl.CostEstimate(
            flops=6 * m * hid * width, bytes_accessed=6 * hid * width, transcendentals=m * hid),
    )(grad, ids, gates, pre, w_gate, w_up, w_down)
    block = min(hid, 256)
    down, out = pl.pallas_call(
        down_kernel,
        grid=(hid // block,),
        out_shape=(
            jax.ShapeDtypeStruct((hid, width), BF16),
            jax.ShapeDtypeStruct((tok, width), BF16),
        ),
        in_specs=[
            pl.BlockSpec((m, block), lambda i: (0, i)),
            pl.BlockSpec((m, width), lambda i: (0, 0)),
            pl.BlockSpec((tok, width), lambda i: (0, 0)),
        ],
        out_specs=(
            pl.BlockSpec((block, width), lambda i: (i, 0)),
            pl.BlockSpec((tok, width), lambda i: (0, 0)),
        ),
        compiler_params=pltpu.CompilerParams(vmem_limit_bytes=48 * 1024 * 1024),
        cost_estimate=pl.CostEstimate(
            flops=2 * m * hid * width, bytes_accessed=2 * hid * width, transcendentals=0),
    )(hidden, rows, passed)
    return (out[None], down[None])


def solution(mesh):
    placed = (
        P("section", "ep", None),
        P("section", "ep", None),
        P("section", "ep", None),
        P("section", "ep", None, None),
        P("ep", None),
        P("ep", None),
        P("ep", None),
    )
    return jax.shard_map(
        on_device,
        mesh=mesh,
        in_specs=placed,
        out_specs=(P("section", "ep", None), P("section", "ep", None)),
        check_vma=False,
    )
```

```python
import functools

import jax
import jax.numpy as jnp
from jax import lax
from jax.experimental import pallas as pl
from jax.experimental.pallas import tpu as pltpu
from jax.sharding import PartitionSpec as P

EXPERTS = 4
SLOT = 3
PAD = 4
FOLD = 4
ROWS = EXPERTS * PAD
WIDE = 896
F32 = jnp.float32
BF16 = jnp.bfloat16


def nt(a, b):
    return lax.dot_general(a, b, (((1,), (1,)), ((), ())), preferred_element_type=F32)


def tn(a, b):
    return lax.dot_general(a, b, (((0,), (0,)), ((), ())), preferred_element_type=F32)


def nn(a, b):
    return lax.dot_general(a, b, (((1,), (0,)), ((), ())), preferred_element_type=F32)


def iota(shape, dim):
    return lax.broadcasted_iota(jnp.int32, shape, dim)


def main_kernel(
    n_dev, n_sec, pieces,
    grad_ref, ids_ref, gates_ref, pre_ref, wg_hbm, wu_hbm, wd_hbm,
    passed_ref, rows_ref, hidden_ref,
    wg, wu, wd, gsend, grecv, xsend, xrecv, zsend, zrecv, gbuf, dh, fg, fu, dgate, dup,
    sel, whi, wlo, perm,
    wd_sem, wg_sem, wu_sem,
    gz_s, gz_r, gx_s, gx_r, rx_s, rx_r, rz_s, rz_r, ps_s, ps_r,
):
    slices = n_dev // EXPERTS
    tok = grad_ref.shape[1]
    w = WIDE
    cw = FOLD * w
    j = lax.axis_index("ep")
    s = lax.axis_index("section")
    e = lax.div(j, slices)
    g = lax.rem(j, slices)

    def cols(p):
        return pl.ds(pl.multiple_of(p * cw, cw), cw)

    def wcopy(hbm, vm, sem, p):
        return pltpu.make_async_copy(hbm.at[:, cols(p)], vm.at[:, cols(p)], sem.at[p])

    barrier = pltpu.get_barrier_semaphore()
    for d in range(1, EXPERTS):
        pl.semaphore_signal(barrier, inc=1, device_id={"ep": lax.rem(e + d, EXPERTS) * slices + g},
                            device_id_type=pl.DeviceIdType.MESH)
    for d in range(1, slices):
        pl.semaphore_signal(barrier, inc=1, device_id={"ep": e * slices + lax.rem(g + d, slices)},
                            device_id_type=pl.DeviceIdType.MESH)

    @pl.when(s > 0)
    def _():
        pl.semaphore_signal(barrier, inc=1, device_id={"section": s - 1},
                            device_id_type=pl.DeviceIdType.MESH)

    @pl.when(s < n_sec - 1)
    def _():
        pl.semaphore_signal(barrier, inc=1, device_id={"section": s + 1},
                            device_id_type=pl.DeviceIdType.MESH)

    def issue_down(p, c):
        wcopy(wd_hbm, wd, wd_sem, p).start()
        return c

    def issue_rest(p, c):
        wcopy(wg_hbm, wg, wg_sem, p).start()
        wcopy(wu_hbm, wu, wu_sem, p).start()
        return c

    lax.fori_loop(0, pieces, issue_down, 0)
    lax.fori_loop(0, pieces, issue_rest, 0)

    ids = ids_ref[0]
    gates = gates_ref[0]
    q = EXPERTS * FOLD * PAD
    qt = FOLD * tok
    named = iota((ROWS, tok), 0)
    member = jnp.zeros((ROWS, tok), F32)
    coef = jnp.zeros((ROWS, tok), F32)
    for c in range(ids.shape[0]):
        eq = ids[c:c + 1, :] == named
        member = member + jnp.where(eq, 1.0, 0.0)
        coef = coef + jnp.where(eq, gates[c:c + 1, :], 0.0)
    tri = jnp.where(iota((tok, tok), 0) <= iota((tok, tok), 1), 1.0, 0.0).astype(BF16)
    rank = nn(member.astype(BF16), tri) - 1.0
    rank = jnp.where(member == 1.0, rank, -1.0).astype(BF16)
    tile = jnp.where(iota((tok, qt), 0) == lax.rem(iota((tok, qt), 1), tok), 1.0, 0.0).astype(BF16)
    rank4 = nn(rank, tile).astype(BF16)
    spread = jnp.where((iota((q, ROWS), 0) >> 4) == iota((q, ROWS), 1), 1.0, 0.0).astype(BF16)
    spread_t = jnp.where(iota((ROWS, q), 0) == (iota((ROWS, q), 1) >> 4), 1.0, 0.0).astype(BF16)
    ri, rj = iota((q, qt), 0), iota((q, qt), 1)
    hit = jnp.logical_and(
        nn(spread, rank4) == (ri & 3).astype(F32),
        jnp.logical_and(((ri >> 2) & 3) == lax.div(rj, tok), (ri & 3) < SLOT),
    )
    sel[...] = jnp.where(hit, 1.0, 0.0).astype(BF16)
    ci, cj = iota((qt, q), 0), iota((qt, q), 1)
    hit_t = jnp.logical_and(
        tn(rank4, spread_t) == (cj & 3).astype(F32),
        jnp.logical_and(((cj >> 2) & 3) == lax.div(ci, tok), (cj & 3) < SLOT),
    )
    high = coef.astype(BF16)
    low = (coef - high.astype(F32)).astype(BF16)
    high4 = nn(high, tile).astype(BF16)
    low4 = nn(low, tile).astype(BF16)
    whi[...] = jnp.where(hit_t, tn(high4, spread_t), 0.0).astype(BF16)
    wlo[...] = jnp.where(hit_t, tn(low4, spread_t), 0.0).astype(BF16)
    fi, fj = iota((q, q), 0), iota((q, q), 1)
    perm[...] = jnp.where(
        jnp.logical_and(
            jnp.logical_and((fi >> 4) == ((fj >> 2) & 3), ((fi >> 2) & 3) == (fj >> 4)),
            (fi & 3) == (fj & 3),
        ),
        1.0, 0.0,
    ).astype(BF16)

    def z_copy(src, dst, ss, rs, p, d):
        to = lax.rem(e + d, EXPERTS)
        return pltpu.make_async_remote_copy(
            src_ref=src.at[p, pl.ds(pl.multiple_of(to * ROWS, ROWS), ROWS)],
            dst_ref=dst.at[p, pl.ds(pl.multiple_of(e * ROWS, ROWS), ROWS)],
            send_sem=ss.at[p, d - 1], recv_sem=rs.at[p, d - 1],
            device_id={"ep": to * slices + g}, device_id_type=pl.DeviceIdType.MESH)

    def z_wait(src, dst, ss, rs, p, d):
        frm = lax.rem(e + EXPERTS - d, EXPERTS)
        spot = pl.ds(pl.multiple_of(frm * ROWS, ROWS), ROWS)
        pltpu.make_async_remote_copy(
            src_ref=src.at[p, spot], dst_ref=dst.at[p, spot],
            send_sem=ss.at[p, d - 1], recv_sem=rs.at[p, d - 1],
            device_id={"ep": frm * slices + g}, device_id_type=pl.DeviceIdType.MESH).wait_recv()

    def gx_copy(p, d, row):
        at = rows_ref.at[pl.ds(pl.multiple_of(row * ROWS, ROWS), ROWS), cols(p)]
        return pltpu.make_async_remote_copy(
            src_ref=at, dst_ref=at, send_sem=gx_s.at[p, d - 1], recv_sem=gx_r.at[p, d - 1],
            device_id={"ep": e * slices + lax.rem(g + d, slices)},
            device_id_type=pl.DeviceIdType.MESH)

    def rx_copy(p, d):
        to = lax.rem(g + d, slices)
        return pltpu.make_async_remote_copy(
            src_ref=xsend.at[p, pl.ds(pl.multiple_of(to * ROWS, ROWS), ROWS)],
            dst_ref=xrecv.at[p, d - 1],
            send_sem=rx_s.at[p, d - 1], recv_sem=rx_r.at[p, d - 1],
            device_id={"ep": e * slices + to}, device_id_type=pl.DeviceIdType.MESH)

    def ps_copy(p):
        return pltpu.make_async_remote_copy(
            src_ref=gbuf.at[:, cols(p)], dst_ref=passed_ref.at[:, cols(p)],
            send_sem=ps_s.at[p], recv_sem=ps_r.at[p],
            device_id={"section": lax.rem(s + n_sec - 1, n_sec)},
            device_id_type=pl.DeviceIdType.MESH)

    mine = pl.ds(pl.multiple_of(e * ROWS, ROWS), ROWS)

    def pick(p, c):
        block = grad_ref[0, :, cols(p)]
        stack = jnp.concatenate([block[:, f * w:(f + 1) * w] for f in range(FOLD)], axis=0)
        gsend[p] = nn(sel[...], stack).astype(BF16)
        grecv[p, mine] = gsend[p, mine]
        return c

    lax.fori_loop(0, pieces, pick, 0)

    neighbours = lax.div(s + n_sec - 1, n_sec) + lax.div(2 * n_sec - 2 - s, n_sec)
    pl.semaphore_wait(barrier, EXPERTS - 1 + slices - 1 + neighbours)

    def send_rows(p, c):
        for d in range(1, EXPERTS):
            z_copy(gsend, grecv, gz_s, gz_r, p, d).start()
        return c

    lax.fori_loop(0, pieces, send_rows, 0)

    m = slices * ROWS
    r = n_dev * SLOT
    pi, pj = iota((m, r), 0), iota((m, r), 1)
    source = (((pi >> 2) & 3) * slices + (pi >> 4)) * SLOT + (pi & 3)
    order = jnp.where(jnp.logical_and(source == pj, (pi & 3) < SLOT), 1.0, 0.0).astype(BF16)
    a = nn(order, pre_ref[0, :, 0, :])
    u = nn(order, pre_ref[0, :, 1, :])
    sig = jax.nn.sigmoid(a)
    swish = a * sig
    hidden_ref[...] = (swish * u).astype(BF16)
    fg[...] = u * sig * (1.0 + a * (1.0 - sig))
    fu[...] = swish
    dh[...] = jnp.zeros_like(dh)

    @pl.when(s == n_sec - 1)
    def _():
        passed_ref[...] = jnp.zeros_like(passed_ref)

    lag = 2

    def gather(p, c):
        @pl.when(p < pieces)
        def _():
            for d in range(1, EXPERTS):
                z_wait(gsend, grecv, gz_s, gz_r, p, d)
            flat = nn(perm[...], grecv[p]).astype(BF16)
            rows_ref[pl.ds(pl.multiple_of(g * ROWS, ROWS), ROWS), cols(p)] = jnp.concatenate(
                [flat[f * ROWS:(f + 1) * ROWS] for f in range(FOLD)], axis=1)
            for d in range(1, slices):
                gx_copy(p, d, g).start()

        @pl.when(p >= lag)
        def _():
            t = p - lag
            for d in range(1, slices):
                gx_copy(t, d, lax.rem(g + slices - d, slices)).wait_recv()
            wcopy(wd_hbm, wd, wd_sem, t).wait()
            dh[...] += nt(rows_ref[:, cols(t)], wd[:, cols(t)])
        return c

    lax.fori_loop(0, pieces + lag, gather, 0)

    d_hidden = dh[...]
    dgate[...] = (d_hidden * fg[...]).astype(BF16)
    dup[...] = (d_hidden * fu[...]).astype(BF16)

    lag_x, lag_z = 1, 3

    def give_back(p, c):
        @pl.when(p < pieces)
        def _():
            wcopy(wg_hbm, wg, wg_sem, p).wait()
            wcopy(wu_hbm, wu, wu_sem, p).wait()
            total = nn(dgate[...], wg[:, cols(p)]) + nn(dup[...], wu[:, cols(p)])
            xsend[p] = total.astype(BF16)
            for d in range(1, slices):
                rx_copy(p, d).start()

        @pl.when(jnp.logical_and(p >= lag_x, p < pieces + lag_x))
        def _():
            t = p - lag_x
            acc = xsend[t, pl.ds(pl.multiple_of(g * ROWS, ROWS), ROWS)].astype(F32)
            for d in range(1, slices):
                rx_copy(t, d).wait_recv()
                acc = acc + xrecv[t, d - 1].astype(F32)
            acc = acc.astype(BF16)
            stack = jnp.concatenate([acc[:, f * w:(f + 1) * w] for f in range(FOLD)], axis=0)
            zsend[t] = nn(perm[...], stack).astype(BF16)
            for d in range(1, EXPERTS):
                z_copy(zsend, zrecv, rz_s, rz_r, t, d).start()
            zrecv[t, mine] = zsend[t, mine]

        @pl.when(p >= lag_z)
        def _():
            t = p - lag_z
            for d in range(1, EXPERTS):
                z_wait(zsend, zrecv, rz_s, rz_r, t, d)
            got = zrecv[t]
            terms = nn(whi[...], got) + nn(wlo[...], got)
            wide = jnp.concatenate([terms[f * tok:(f + 1) * tok] for f in range(FOLD)], axis=1)
            gbuf[:, cols(t)] = (grad_ref[0, :, cols(t)].astype(F32) + wide).astype(BF16)

            @pl.when(s > 0)
            def _():
                ps_copy(t).start()
        return c

    lax.fori_loop(0, pieces + lag_z, give_back, 0)

    def drain(p, c):
        for d in range(1, EXPERTS):
            z_copy(gsend, grecv, gz_s, gz_r, p, d).wait_send()
            z_copy(zsend, zrecv, rz_s, rz_r, p, d).wait_send()
        for d in range(1, slices):
            gx_copy(p, d, g).wait_send()
            rx_copy(p, d).wait_send()

        @pl.when(s < n_sec - 1)
        def _():
            ps_copy(p).wait_recv()

        @pl.when(s > 0)
        def _():
            ps_copy(p).wait_send()
        return c

    lax.fori_loop(0, pieces, drain, 0)


def down_kernel(hidden_ref, rows_ref, passed_ref, down_ref, out_ref):
    @pl.when(pl.program_id(0) == 0)
    def _():
        out_ref[...] = passed_ref[...]

    step = FOLD * WIDE
    h = hidden_ref[...]
    for c in range(rows_ref.shape[1] // step):
        down_ref[:, c * step:(c + 1) * step] = tn(h, rows_ref[:, c * step:(c + 1) * step]).astype(BF16)


def on_device(grad, ids, gates, pre, w_gate, w_up, w_down):
    n_dev = lax.axis_size("ep")
    n_sec = lax.axis_size("section")
    slices = n_dev // EXPERTS
    tok, width = grad.shape[1:]
    hid = w_down.shape[0]
    pieces = width // (FOLD * WIDE)
    m = slices * ROWS
    q = EXPERTS * FOLD * PAD
    qt = FOLD * tok
    vmem = pl.BlockSpec(memory_space=pltpu.VMEM)
    hbm = pl.BlockSpec(memory_space=pl.ANY)
    dma = pltpu.SemaphoreType.DMA
    x_n = slices - 1
    z_n = EXPERTS - 1
    passed, rows, hidden = pl.pallas_call(
        functools.partial(main_kernel, n_dev, n_sec, pieces),
        out_shape=(
            jax.ShapeDtypeStruct((tok, width), BF16),
            jax.ShapeDtypeStruct((m, width), BF16),
            jax.ShapeDtypeStruct((m, hid), BF16),
        ),
        in_specs=[vmem, vmem, vmem, vmem, hbm, hbm, hbm],
        out_specs=(vmem, vmem, vmem),
        scratch_shapes=[
            pltpu.VMEM((hid, width), BF16),
            pltpu.VMEM((hid, width), BF16),
            pltpu.VMEM((hid, width), BF16),
            pltpu.VMEM((pieces, q, WIDE), BF16),
            pltpu.VMEM((pieces, q, WIDE), BF16),
            pltpu.VMEM((pieces, m, FOLD * WIDE), BF16),
            pltpu.VMEM((pieces, x_n, ROWS, FOLD * WIDE), BF16),
            pltpu.VMEM((pieces, q, WIDE), BF16),
            pltpu.VMEM((pieces, q, WIDE), BF16),
            pltpu.VMEM((tok, width), BF16),
            pltpu.VMEM((m, hid), F32),
            pltpu.VMEM((m, hid), F32),
            pltpu.VMEM((m, hid), F32),
            pltpu.VMEM((m, hid), BF16),
            pltpu.VMEM((m, hid), BF16),
            pltpu.VMEM((q, qt), BF16),
            pltpu.VMEM((qt, q), BF16),
            pltpu.VMEM((qt, q), BF16),
            pltpu.VMEM((q, q), BF16),
            dma((pieces,)), dma((pieces,)), dma((pieces,)),
            dma((pieces, z_n)), dma((pieces, z_n)),
            dma((pieces, x_n)), dma((pieces, x_n)),
            dma((pieces, x_n)), dma((pieces, x_n)),
            dma((pieces, z_n)), dma((pieces, z_n)),
            dma((pieces,)), dma((pieces,)),
        ],
        compiler_params=pltpu.CompilerParams(
            collective_id=0, has_side_effects=True, vmem_limit_bytes=60 * 1024 * 1024),
        cost_estimate=pl.CostEstimate(
            flops=6 * m * hid * width, bytes_accessed=6 * hid * width, transcendentals=m * hid),
    )(grad, jnp.swapaxes(ids, 1, 2), jnp.swapaxes(gates, 1, 2), pre, w_gate, w_up, w_down)
    block = min(hid, 128)
    down, out = pl.pallas_call(
        down_kernel,
        grid=(hid // block,),
        out_shape=(
            jax.ShapeDtypeStruct((hid, width), BF16),
            jax.ShapeDtypeStruct((tok, width), BF16),
        ),
        in_specs=[
            pl.BlockSpec((m, block), lambda i: (0, i)),
            pl.BlockSpec((m, width), lambda i: (0, 0)),
            pl.BlockSpec((tok, width), lambda i: (0, 0)),
        ],
        out_specs=(
            pl.BlockSpec((block, width), lambda i: (i, 0)),
            pl.BlockSpec((tok, width), lambda i: (0, 0)),
        ),
        compiler_params=pltpu.CompilerParams(vmem_limit_bytes=60 * 1024 * 1024),
        cost_estimate=pl.CostEstimate(
            flops=2 * m * hid * width, bytes_accessed=2 * hid * width, transcendentals=0),
    )(hidden, rows, passed)
    return (out[None], down[None])


def solution(mesh):
    placed = (
        P("section", "ep", None),
        P("section", "ep", None),
        P("section", "ep", None),
        P("section", "ep", None, None),
        P("ep", None),
        P("ep", None),
        P("ep", None),
    )
    return jax.shard_map(
        on_device,
        mesh=mesh,
        in_specs=placed,
        out_specs=(P("section", "ep", None), P("section", "ep", None)),
        check_vma=False,
    )
```

```python
import functools

import jax
import jax.numpy as jnp
from jax import lax
from jax.experimental import pallas as pl
from jax.experimental.pallas import tpu as pltpu
from jax.sharding import PartitionSpec as P

EXPERTS = 4
SLOT = 3
PAD = 4
FOLD = 4
ROWS = EXPERTS * PAD
UNIT = 512
GATHER_PIECES = 3
RETURN_PIECES = 4
F32 = jnp.float32
BF16 = jnp.bfloat16


def nt(a, b):
    return lax.dot_general(a, b, (((1,), (1,)), ((), ())), preferred_element_type=F32)


def tn(a, b):
    return lax.dot_general(a, b, (((0,), (0,)), ((), ())), preferred_element_type=F32)


def nn(a, b):
    return lax.dot_general(a, b, (((1,), (0,)), ((), ())), preferred_element_type=F32)


def split(width, count):
    units = width // UNIT
    sizes = [UNIT * (units // count + (1 if i < units % count else 0)) for i in range(count)]
    return [(sum(sizes[:i]), size) for i, size in enumerate(sizes)]


def iota(shape, dim):
    return lax.broadcasted_iota(jnp.int32, shape, dim)


def main_kernel(
    n_dev, n_sec, gp, rp,
    grad_ref, ids_ref, gates_ref, pre_ref, wg_hbm, wu_hbm, wd_hbm,
    passed_ref, rows_ref, hidden_ref,
    wg, wu, wd, gsend, grecv, xsend, xrecv, zsend, zrecv, gbuf, dh, fg, fu, dgate, dup,
    sel, whi, wlo, perm,
    wd_sem, wg_sem, wu_sem,
    gz_s, gz_r, gx_s, gx_r, rx_s, rx_r, rz_s, rz_r, ps_s, ps_r,
):
    slices = n_dev // EXPERTS
    tok = grad_ref.shape[1]
    j = lax.axis_index("ep")
    s = lax.axis_index("section")
    e = lax.div(j, slices)
    g = lax.rem(j, slices)

    def cols(pc):
        return pl.ds(pc[0], pc[1])

    def narrow(pc):
        return pl.ds(pc[0] // FOLD, pc[1] // FOLD)

    def folded(x, pc):
        w = pc[1] // FOLD
        return jnp.concatenate([x[:, f * w:(f + 1) * w] for f in range(FOLD)], axis=0)

    def unfolded(x, rows):
        return jnp.concatenate([x[f * rows:(f + 1) * rows] for f in range(FOLD)], axis=1)

    def wcopy(hbm, vm, sem, i, pc):
        return pltpu.make_async_copy(hbm.at[:, cols(pc)], vm.at[:, cols(pc)], sem.at[i])

    barrier = pltpu.get_barrier_semaphore()
    for d in range(1, EXPERTS):
        pl.semaphore_signal(barrier, inc=1, device_id={"ep": lax.rem(e + d, EXPERTS) * slices + g},
                            device_id_type=pl.DeviceIdType.MESH)
    for d in range(1, slices):
        pl.semaphore_signal(barrier, inc=1, device_id={"ep": e * slices + lax.rem(g + d, slices)},
                            device_id_type=pl.DeviceIdType.MESH)

    @pl.when(s > 0)
    def _():
        pl.semaphore_signal(barrier, inc=1, device_id={"section": s - 1},
                            device_id_type=pl.DeviceIdType.MESH)

    @pl.when(s < n_sec - 1)
    def _():
        pl.semaphore_signal(barrier, inc=1, device_id={"section": s + 1},
                            device_id_type=pl.DeviceIdType.MESH)

    for i, pc in enumerate(gp):
        wcopy(wd_hbm, wd, wd_sem, i, pc).start()
    for i, pc in enumerate(rp):
        wcopy(wg_hbm, wg, wg_sem, i, pc).start()
        wcopy(wu_hbm, wu, wu_sem, i, pc).start()

    ids = ids_ref[0]
    gates = gates_ref[0]
    q = EXPERTS * FOLD * PAD
    qt = FOLD * tok
    named = iota((ROWS, tok), 0)
    member = jnp.zeros((ROWS, tok), F32)
    coef = jnp.zeros((ROWS, tok), F32)
    for c in range(ids.shape[0]):
        eq = ids[c:c + 1, :] == named
        member = member + jnp.where(eq, 1.0, 0.0)
        coef = coef + jnp.where(eq, gates[c:c + 1, :], 0.0)
    tri = jnp.where(iota((tok, tok), 0) <= iota((tok, tok), 1), 1.0, 0.0).astype(BF16)
    rank = nn(member.astype(BF16), tri) - 1.0
    rank = jnp.where(member == 1.0, rank, -1.0).astype(BF16)
    tile = jnp.where(iota((tok, qt), 0) == lax.rem(iota((tok, qt), 1), tok), 1.0, 0.0).astype(BF16)
    rank4 = nn(rank, tile).astype(BF16)
    spread = jnp.where((iota((q, ROWS), 0) >> 4) == iota((q, ROWS), 1), 1.0, 0.0).astype(BF16)
    spread_t = jnp.where(iota((ROWS, q), 0) == (iota((ROWS, q), 1) >> 4), 1.0, 0.0).astype(BF16)
    ri, rj = iota((q, qt), 0), iota((q, qt), 1)
    hit = jnp.logical_and(
        nn(spread, rank4) == (ri & 3).astype(F32),
        jnp.logical_and(((ri >> 2) & 3) == lax.div(rj, tok), (ri & 3) < SLOT),
    )
    sel[...] = jnp.where(hit, 1.0, 0.0).astype(BF16)
    ci, cj = iota((qt, q), 0), iota((qt, q), 1)
    hit_t = jnp.logical_and(
        tn(rank4, spread_t) == (cj & 3).astype(F32),
        jnp.logical_and(((cj >> 2) & 3) == lax.div(ci, tok), (cj & 3) < SLOT),
    )
    high = coef.astype(BF16)
    low = (coef - high.astype(F32)).astype(BF16)
    high4 = nn(high, tile).astype(BF16)
    low4 = nn(low, tile).astype(BF16)
    whi[...] = jnp.where(hit_t, tn(high4, spread_t), 0.0).astype(BF16)
    wlo[...] = jnp.where(hit_t, tn(low4, spread_t), 0.0).astype(BF16)
    fi, fj = iota((q, q), 0), iota((q, q), 1)
    perm[...] = jnp.where(
        jnp.logical_and(
            jnp.logical_and((fi >> 4) == ((fj >> 2) & 3), ((fi >> 2) & 3) == (fj >> 4)),
            (fi & 3) == (fj & 3),
        ),
        1.0, 0.0,
    ).astype(BF16)

    def block(i):
        return pl.ds(pl.multiple_of(i * ROWS, ROWS), ROWS)

    def z_copy(src, dst, ss, rs, i, pc, d):
        to = lax.rem(e + d, EXPERTS)
        return pltpu.make_async_remote_copy(
            src_ref=src.at[block(to), narrow(pc)], dst_ref=dst.at[block(e), narrow(pc)],
            send_sem=ss.at[i, d - 1], recv_sem=rs.at[i, d - 1],
            device_id={"ep": to * slices + g}, device_id_type=pl.DeviceIdType.MESH)

    def z_wait(src, dst, ss, rs, i, pc, d):
        frm = lax.rem(e + EXPERTS - d, EXPERTS)
        pltpu.make_async_remote_copy(
            src_ref=src.at[block(frm), narrow(pc)], dst_ref=dst.at[block(frm), narrow(pc)],
            send_sem=ss.at[i, d - 1], recv_sem=rs.at[i, d - 1],
            device_id={"ep": frm * slices + g}, device_id_type=pl.DeviceIdType.MESH).wait_recv()

    def gx_copy(i, pc, d, row):
        at = rows_ref.at[block(row), cols(pc)]
        return pltpu.make_async_remote_copy(
            src_ref=at, dst_ref=at, send_sem=gx_s.at[i, d - 1], recv_sem=gx_r.at[i, d - 1],
            device_id={"ep": e * slices + lax.rem(g + d, slices)},
            device_id_type=pl.DeviceIdType.MESH)

    def rx_copy(i, pc, d):
        to = lax.rem(g + d, slices)
        return pltpu.make_async_remote_copy(
            src_ref=xsend.at[block(to), cols(pc)], dst_ref=xrecv.at[d - 1, :, cols(pc)],
            send_sem=rx_s.at[i, d - 1], recv_sem=rx_r.at[i, d - 1],
            device_id={"ep": e * slices + to}, device_id_type=pl.DeviceIdType.MESH)

    def ps_copy(i, pc):
        return pltpu.make_async_remote_copy(
            src_ref=gbuf.at[:, cols(pc)], dst_ref=passed_ref.at[:, cols(pc)],
            send_sem=ps_s.at[i], recv_sem=ps_r.at[i],
            device_id={"section": lax.rem(s + n_sec - 1, n_sec)},
            device_id_type=pl.DeviceIdType.MESH)

    neighbours = lax.div(s + n_sec - 1, n_sec) + lax.div(2 * n_sec - 2 - s, n_sec)
    pl.semaphore_wait(barrier, EXPERTS - 1 + slices - 1 + neighbours)

    for i, pc in enumerate(gp):
        gsend[:, narrow(pc)] = nn(sel[...], folded(grad_ref[0, :, cols(pc)], pc)).astype(BF16)
        for d in range(1, EXPERTS):
            z_copy(gsend, grecv, gz_s, gz_r, i, pc, d).start()
        grecv[block(e), narrow(pc)] = gsend[block(e), narrow(pc)]

    m = slices * ROWS
    r = n_dev * SLOT
    pi, pj = iota((m, r), 0), iota((m, r), 1)
    source = (((pi >> 2) & 3) * slices + (pi >> 4)) * SLOT + (pi & 3)
    order = jnp.where(jnp.logical_and(source == pj, (pi & 3) < SLOT), 1.0, 0.0).astype(BF16)
    a = nn(order, pre_ref[0, :, 0, :])
    u = nn(order, pre_ref[0, :, 1, :])
    sig = jax.nn.sigmoid(a)
    swish = a * sig
    hidden_ref[...] = (swish * u).astype(BF16)
    fg[...] = u * sig * (1.0 + a * (1.0 - sig))
    fu[...] = swish
    dh[...] = jnp.zeros_like(dh)

    @pl.when(s == n_sec - 1)
    def _():
        passed_ref[...] = jnp.zeros_like(passed_ref)

    def take(i, pc):
        for d in range(1, EXPERTS):
            z_wait(gsend, grecv, gz_s, gz_r, i, pc, d)
        flat = nn(perm[...], grecv[:, narrow(pc)]).astype(BF16)
        rows_ref[block(g), cols(pc)] = unfolded(flat, ROWS)
        for d in range(1, slices):
            gx_copy(i, pc, d, g).start()

    def project(i, pc):
        for d in range(1, slices):
            gx_copy(i, pc, d, lax.rem(g + slices - d, slices)).wait_recv()
        wcopy(wd_hbm, wd, wd_sem, i, pc).wait()
        dh[...] += nt(rows_ref[:, cols(pc)], wd[:, cols(pc)])

    lag = 2
    for i in range(len(gp) + lag):
        if i < len(gp):
            take(i, gp[i])
        if i >= lag:
            project(i - lag, gp[i - lag])

    d_hidden = dh[...]
    dgate[...] = (d_hidden * fg[...]).astype(BF16)
    dup[...] = (d_hidden * fu[...]).astype(BF16)

    def multiply(i, pc):
        wcopy(wg_hbm, wg, wg_sem, i, pc).wait()
        wcopy(wu_hbm, wu, wu_sem, i, pc).wait()
        total = nn(dgate[...], wg[:, cols(pc)]) + nn(dup[...], wu[:, cols(pc)])
        xsend[:, cols(pc)] = total.astype(BF16)
        for d in range(1, slices):
            rx_copy(i, pc, d).start()

    def add_pair(i, pc):
        acc = xsend[block(g), cols(pc)].astype(F32)
        for d in range(1, slices):
            rx_copy(i, pc, d).wait_recv()
            acc = acc + xrecv[d - 1, :, cols(pc)].astype(F32)
        zsend[:, narrow(pc)] = nn(perm[...], folded(acc.astype(BF16), pc)).astype(BF16)
        for d in range(1, EXPERTS):
            z_copy(zsend, zrecv, rz_s, rz_r, i, pc, d).start()
        zrecv[block(e), narrow(pc)] = zsend[block(e), narrow(pc)]

    def combine(i, pc):
        for d in range(1, EXPERTS):
            z_wait(zsend, zrecv, rz_s, rz_r, i, pc, d)
        got = zrecv[:, narrow(pc)]
        terms = nn(whi[...], got) + nn(wlo[...], got)
        gbuf[:, cols(pc)] = (grad_ref[0, :, cols(pc)].astype(F32) + unfolded(terms, tok)).astype(BF16)

        @pl.when(s > 0)
        def _():
            ps_copy(i, pc).start()

    lag_x, lag_z = 1, 3
    for i in range(len(rp) + lag_z):
        if i < len(rp):
            multiply(i, rp[i])
        if lag_x <= i < len(rp) + lag_x:
            add_pair(i - lag_x, rp[i - lag_x])
        if i >= lag_z:
            combine(i - lag_z, rp[i - lag_z])

    for i, pc in enumerate(gp):
        for d in range(1, EXPERTS):
            z_copy(gsend, grecv, gz_s, gz_r, i, pc, d).wait_send()
        for d in range(1, slices):
            gx_copy(i, pc, d, g).wait_send()
    for i, pc in enumerate(rp):
        for d in range(1, EXPERTS):
            z_copy(zsend, zrecv, rz_s, rz_r, i, pc, d).wait_send()
        for d in range(1, slices):
            rx_copy(i, pc, d).wait_send()

    @pl.when(s < n_sec - 1)
    def _():
        for i, pc in enumerate(rp):
            ps_copy(i, pc).wait_recv()

    @pl.when(s > 0)
    def _():
        for i, pc in enumerate(rp):
            ps_copy(i, pc).wait_send()


def down_kernel(hidden_ref, rows_ref, passed_ref, down_ref, out_ref):
    @pl.when(pl.program_id(0) == 0)
    def _():
        out_ref[...] = passed_ref[...]

    step = 2 * UNIT
    h = hidden_ref[...]
    for c in range(rows_ref.shape[1] // step):
        down_ref[:, c * step:(c + 1) * step] = tn(h, rows_ref[:, c * step:(c + 1) * step]).astype(BF16)


def on_device(grad, ids, gates, pre, w_gate, w_up, w_down):
    n_dev = lax.axis_size("ep")
    n_sec = lax.axis_size("section")
    slices = n_dev // EXPERTS
    tok, width = grad.shape[1:]
    hid = w_down.shape[0]
    gp, rp = split(width, GATHER_PIECES), split(width, RETURN_PIECES)
    g_n, r_n = len(gp), len(rp)
    m = slices * ROWS
    q = EXPERTS * FOLD * PAD
    qt = FOLD * tok
    vmem = pl.BlockSpec(memory_space=pltpu.VMEM)
    hbm = pl.BlockSpec(memory_space=pl.ANY)
    dma = pltpu.SemaphoreType.DMA
    x_n = slices - 1
    z_n = EXPERTS - 1
    passed, rows, hidden = pl.pallas_call(
        functools.partial(main_kernel, n_dev, n_sec, gp, rp),
        out_shape=(
            jax.ShapeDtypeStruct((tok, width), BF16),
            jax.ShapeDtypeStruct((m, width), BF16),
            jax.ShapeDtypeStruct((m, hid), BF16),
        ),
        in_specs=[vmem, vmem, vmem, vmem, hbm, hbm, hbm],
        out_specs=(vmem, vmem, vmem),
        scratch_shapes=[
            pltpu.VMEM((hid, width), BF16),
            pltpu.VMEM((hid, width), BF16),
            pltpu.VMEM((hid, width), BF16),
            pltpu.VMEM((q, width // FOLD), BF16),
            pltpu.VMEM((q, width // FOLD), BF16),
            pltpu.VMEM((m, width), BF16),
            pltpu.VMEM((x_n, ROWS, width), BF16),
            pltpu.VMEM((q, width // FOLD), BF16),
            pltpu.VMEM((q, width // FOLD), BF16),
            pltpu.VMEM((tok, width), BF16),
            pltpu.VMEM((m, hid), F32),
            pltpu.VMEM((m, hid), F32),
            pltpu.VMEM((m, hid), F32),
            pltpu.VMEM((m, hid), BF16),
            pltpu.VMEM((m, hid), BF16),
            pltpu.VMEM((q, qt), BF16),
            pltpu.VMEM((qt, q), BF16),
            pltpu.VMEM((qt, q), BF16),
            pltpu.VMEM((q, q), BF16),
            dma((g_n,)), dma((r_n,)), dma((r_n,)),
            dma((g_n, z_n)), dma((g_n, z_n)),
            dma((g_n, x_n)), dma((g_n, x_n)),
            dma((r_n, x_n)), dma((r_n, x_n)),
            dma((r_n, z_n)), dma((r_n, z_n)),
            dma((r_n,)), dma((r_n,)),
        ],
        compiler_params=pltpu.CompilerParams(
            collective_id=0, has_side_effects=True, vmem_limit_bytes=60 * 1024 * 1024),
        cost_estimate=pl.CostEstimate(
            flops=6 * m * hid * width, bytes_accessed=6 * hid * width, transcendentals=m * hid),
    )(grad, jnp.swapaxes(ids, 1, 2), jnp.swapaxes(gates, 1, 2), pre, w_gate, w_up, w_down)
    block = min(hid, 256)
    down, out = pl.pallas_call(
        down_kernel,
        grid=(hid // block,),
        out_shape=(
            jax.ShapeDtypeStruct((hid, width), BF16),
            jax.ShapeDtypeStruct((tok, width), BF16),
        ),
        in_specs=[
            pl.BlockSpec((m, block), lambda i: (0, i)),
            pl.BlockSpec((m, width), lambda i: (0, 0)),
            pl.BlockSpec((tok, width), lambda i: (0, 0)),
        ],
        out_specs=(
            pl.BlockSpec((block, width), lambda i: (i, 0)),
            pl.BlockSpec((tok, width), lambda i: (0, 0)),
        ),
        compiler_params=pltpu.CompilerParams(vmem_limit_bytes=60 * 1024 * 1024),
        cost_estimate=pl.CostEstimate(
            flops=2 * m * hid * width, bytes_accessed=2 * hid * width, transcendentals=0),
    )(hidden, rows, passed)
    return (out[None], down[None])


def solution(mesh):
    placed = (
        P("section", "ep", None),
        P("section", "ep", None),
        P("section", "ep", None),
        P("section", "ep", None, None),
        P("ep", None),
        P("ep", None),
        P("ep", None),
    )
    return jax.shard_map(
        on_device,
        mesh=mesh,
        in_specs=placed,
        out_specs=(P("section", "ep", None), P("section", "ep", None)),
        check_vma=False,
    )
```
